512 devices in a mesh: ia: 16 (over x, z_hi, core), ja: 32 (over y, z_lo).
Axes of the slice: x: 4, y: 4, z: 16 (z_hi: 2, z_lo: 8; z = z_hi * 8 + z_lo), core: 2. Of those that a mesh axis runs over, the one named last changes fastest.
Arguments:
- amplitudes: bfloat16 [64, 64, 64, 384], P('ia', 'ja'), may hold values from -6 to 6
- integrals: bfloat16 [64, 64, 64, 384], P('ja', 'ia'), may hold values from -0.078125 to 0.078125
Outputs:
- cycle_term: bfloat16 [64, 64, 4096], P('ia', 'ja')
The draws below stay inside these ranges and needn't reach their ends.
All inputs are finite; a program needn't handle non-finite values.
Results may differ from the reference program's by a relative error of at most 0.0011.
Values may be sent and summed in bfloat16 or wider, within the bound.
A program may use at most 64 MiB of HBM per device.

```python
import jax
import jax.numpy as jnp
from jax import lax

O = 64
V = 384
VA = 64


def spiked(result, stream_key, source, target, shards_of, factor):
    def block_of(position):
        return (jnp.arange(result.shape[position]) // (result.shape[position] // shards_of)).reshape((-1,) + (1,) * (result.ndim - 1 - position))

    first = jax.random.permutation(stream_key, shards_of)[block_of(target)]
    far = (block_of(target) + shards_of // 2) % shards_of
    return jnp.where((block_of(source) == first) | (block_of(source) == far), factor * result, result)


def level_of(key, shape, cuts, low, top_value):
    loudness, own = 1.0, jax.random.fold_in(key, 6)
    for position, shards_of in cuts:
        heights = jnp.exp(jax.random.uniform(jax.random.fold_in(own, position), (shards_of,), jnp.float32, low / len(cuts), top_value / len(cuts)))
        loudness = loudness * jnp.repeat(heights, shape[position] // shards_of).reshape([-1 if axis == position else 1 for axis in range(len(shape))])
    return loudness


def bell_draw(rng, dims, deviation, limit, shards=(), kind=jnp.bfloat16):
    gain = level_of(rng, dims, shards, -0.22, 0.18) if shards else 1.0
    result = jax.random.normal(rng, dims, jnp.float32) * deviation * gain
    return jnp.minimum(jnp.maximum(result, -limit), limit).astype(kind)


def heavy_noise(stream_key, dims, spread, limit, cuts, heavy, kind=jnp.bfloat16):
    entries = spread * jax.random.normal(stream_key, dims, jnp.float32)
    if cuts:
        entries = entries * level_of(stream_key, dims, cuts, -0.22, 0.18)
    return jnp.clip(spiked(entries, jax.random.fold_in(stream_key, 3), *heavy), -limit, limit).astype(kind)


def setup_inputs(seed: int = 0) -> dict:
    key_list = jax.random.split(jax.random.key(seed), 3)
    return {
        "amplitudes": bell_draw(key_list[0], (O, O, VA, V), 1.0, 6.0, ((0, 16), (1, 32))),
        "integrals": heavy_noise(key_list[1], (O, O, VA, V), (O * V) ** -0.5, 0.078125, ((0, 32), (1, 16)), (0, 1, 32, 2.75)),
    }


def reference(amplitudes, integrals):
    left = amplitudes.astype(jnp.float32)
    right = integrals.astype(jnp.float32)
    direct = jnp.einsum("ikac,kjbc->ijab", left, right, precision=lax.Precision.HIGHEST)
    mixed = direct + jnp.transpose(direct, (1, 0, 3, 2))
    return mixed.reshape(O, O, VA * VA).astype(jnp.bfloat16)
```

```python
import functools

import jax
import jax.numpy as jnp
from jax import lax
from jax.experimental import pallas as pl
from jax.experimental.pallas import tpu as pltpu
from jax.sharding import PartitionSpec as P

MESH = pl.DeviceIdType.MESH
F32 = jnp.float32


def place():
    ia, ja = lax.axis_index("ia"), lax.axis_index("ja")
    return ia // 4, ja // 8, (ia // 2) % 2, ja % 8, ia % 2


def device(x, y, zh, zl, c):
    return (x * 4 + zh * 2 + c, y * 8 + zl)


NAMES = (
    ["a1", "a2", "a3", "w"]
    + [f"{n}{r}{q}" for n in ("cross", "fwd") for r in range(2) for q in range(2)]
    + [f"{n}{s}" for n in ("m1p", "m1m", "m2p", "m2m", "m3p", "m3m", "z1", "z2") for s in range(4)]
    + [f"{n}{r}" for n in ("z4", "sw", "ta", "tb") for r in range(2)]
)
INDEX = {name: n for n, name in enumerate(NAMES)}


def kernel(a_ref, w_ref, o_ref, abuf, wbuf, t, m1, m2, m3, sum3, e, z1, f, z2, g, z4, gsum, drecv, rt, ss, rs, ls):
    x, y, zh, zl, c = place()
    b2, b1, b0 = zl // 4, (zl // 2) % 2, zl % 2
    keep = (b2 + zh) % 2
    diagonal = x == y
    local = jnp.logical_and(b2 == zh, b1 == c)

    def up(n, by):
        return (n + by) % 4

    a_to = [device(up(x, d), y, zh, zl, c) for d in (1, 2, 3)]
    sibling = device(x, y, zh, zl, 1 - c)
    anti = device(x, y, 1 - zh, zl, c)
    y_up, y_down = device(x, up(y, 1), zh, zl, c), device(x, up(y, 3), zh, zl, c)
    near = device(x, y, zh, b2 * 4 + b1 * 2 + 1 - b0, c)
    next_pair = device(x, y, zh, b2 * 4 + (1 - b1) * 2 + b0, c)
    far = device(x, y, zh, (1 - b2) * 4 + b1 * 2 + b0, c)
    swap = device(y, x, zh, zl, c)
    t_to = [device(x, y, b2, zh * 4 + c * 2 + q, b1) for q in range(2)]

    barrier = pltpu.get_barrier_semaphore()

    def greet(target):
        pl.semaphore_signal(barrier, inc=1, device_id=target, device_id_type=MESH)

    for target in a_to + [sibling, anti, y_up, y_down, near, next_pair, far]:
        greet(target)

    @pl.when(jnp.logical_not(diagonal))
    def _():
        greet(swap)

    for q in range(2):

        @pl.when(jnp.logical_not(jnp.logical_and(local, b0 == q)))
        def _():
            greet(t_to[q])

    pl.semaphore_wait(barrier, 12 + jnp.where(diagonal, 0, 1) - jnp.where(local, 1, 0))

    def copy(name, src, dst, target):
        n = INDEX[name]
        return pltpu.make_async_remote_copy(
            src_ref=src, dst_ref=dst, send_sem=ss.at[n], recv_sem=rs.at[n], device_id=target, device_id_type=MESH
        )

    cross = {}
    for r in range(2):
        for q in range(2):
            j = 2 * q + r
            cross[r, q] = copy(f"cross{r}{q}", w_ref.at[:, j], wbuf.at[1, c, :, j], anti)
            cross[r, q].start()
    sends = [copy(f"a{n + 1}", a_ref, abuf.at[x], a_to[n]) for n in range(3)]
    sends.append(copy("w", w_ref, wbuf.at[0, c], sibling))
    for one in sends:
        one.start()
    own_a = pltpu.make_async_copy(a_ref, abuf.at[x], ls.at[0])
    own_w = pltpu.make_async_copy(w_ref, wbuf.at[0, c], ls.at[1])
    own_a.start()
    own_w.start()
    own_a.wait()
    own_w.wait()
    for one in sends:
        one.wait()

    def product(s):
        sel, r = s // 2, s % 2

        def one(n, _):
            total = None
            for k in range(2):
                left = jnp.concatenate([wbuf[sel, cj, k, 2 * q + r] for cj in range(2) for q in range(2)], axis=0)
                right = abuf[n, :, k].reshape(256, 384)
                part = lax.dot_general(left, right, (((1,), (1,)), ((), ())), preferred_element_type=F32)
                total = part if total is None else total + part
            t[s, n] = total
            return 0

        lax.fori_loop(0, 4, one, 0)

    low, high = pl.ds(0, 128), pl.ds(128, 128)
    live = {}

    def begin(name, *rest):
        live[name] = copy(name, *rest)
        live[name].start()

    def y_start(s):
        begin(f"m1p{s}", t.at[s, up(y, 2), low], m1.at[s, 0], y_up)
        begin(f"m1m{s}", t.at[s, up(y, 2), high], m1.at[s, 1], y_down)
        begin(f"m2p{s}", t.at[s, up(y, 1), high], m2.at[s, 0], y_up)
        begin(f"m2m{s}", t.at[s, up(y, 3), low], m2.at[s, 1], y_down)

    def y_pass(s):
        live[f"m1p{s}"].wait()
        sum3[s, 0] = m1[s, 0] + t[s, up(y, 1), low]
        begin(f"m3p{s}", sum3.at[s, 0], m3.at[s, 0], y_up)
        live[f"m1m{s}"].wait()
        sum3[s, 1] = m1[s, 1] + t[s, up(y, 3), high]
        begin(f"m3m{s}", sum3.at[s, 1], m3.at[s, 1], y_down)

    def y_end(s):
        for name in ("m2p", "m2m", "m3p", "m3m"):
            live[f"{name}{s}"].wait()
        e[s, 0] = (t[s, y, low] + m3[s, 0] + m2[s, 1]).reshape(2, 64, 256)
        e[s, 1] = (t[s, y, high] + m2[s, 0] + m3[s, 1]).reshape(2, 64, 256)
        begin(f"z1{s}", e.at[s, :, 1 - b0], z1.at[s], near)

    def z_second(s):
        live[f"z1{s}"].wait()
        f[s] = e[s, :, b0] + z1[s]
        begin(f"z2{s}", f.at[s, 1 - b1], z2.at[s], next_pair)

    def z_third(s):
        sel, r = s // 2, s % 2
        live[f"z2{s}"].wait()
        g[r, sel] = f[s, b1] + z2[s]

        @pl.when(keep != sel)
        def _():
            copy(f"z4{r}", g.at[r, sel], z4.at[r], far).start()

    def last(r):
        copy(f"z4{r}", g.at[r, 0], z4.at[r], far).wait()
        gsum[r] = g[r, keep] + z4[r]

        @pl.when(diagonal)
        def _():
            drecv[r] = gsum[r]

        @pl.when(jnp.logical_not(diagonal))
        def _():
            copy(f"sw{r}", gsum.at[r], drecv.at[r], swap).start()

        for q in range(2):
            piece = gsum.at[r, :, pl.ds(q * 128, 128)]
            itself = jnp.logical_and(local, b0 == q)

            @pl.when(itself)
            def _():
                rt[b0, r] = piece[...]

            @pl.when(jnp.logical_not(itself))
            def _():
                n = INDEX[f"t{'ab'[q]}{r}"]
                pltpu.make_async_remote_copy(
                    src_ref=piece,
                    dst_ref=rt.at[b0, r],
                    send_sem=ss.at[n],
                    recv_sem=rs.at[INDEX[f"ta{r}"] + 2 * b0],
                    device_id=t_to[q],
                    device_id_type=MESH,
                ).start()

    def finish(r):
        @pl.when(jnp.logical_not(diagonal))
        def _():
            copy(f"sw{r}", gsum.at[r], drecv.at[r], swap).wait()

        for q in range(2):
            piece = gsum.at[r, :, pl.ds(q * 128, 128)]

            @pl.when(jnp.logical_not(jnp.logical_and(local, b0 == q)))
            def _():
                copy(f"t{'ab'[q]}{r}", piece, rt.at[q, r], t_to[q]).wait()

    def arrive(r):
        for q in range(2):
            j = 2 * q + r
            cross[r, q].wait()
            begin(f"fwd{r}{q}", wbuf.at[1, c, :, j], wbuf.at[1, c, :, j], sibling)

    def shared(r):
        for q in range(2):
            live[f"fwd{r}{q}"].wait()

    product(0)
    y_start(0)
    product(1)
    y_start(1)
    y_pass(0)
    y_pass(1)
    y_end(0)
    arrive(0)
    shared(0)
    product(2)
    y_start(2)
    y_end(1)
    z_second(0)
    z_second(1)
    y_pass(2)
    arrive(1)
    shared(1)
    product(3)
    y_start(3)
    z_third(0)
    z_third(1)
    y_end(2)
    y_pass(3)
    z_second(2)
    y_end(3)
    z_third(2)
    last(0)
    z_second(3)
    z_third(3)
    last(1)
    finish(0)
    finish(1)
    d = jnp.transpose(drecv[...].reshape(128, 256))
    o_ref[...] = (d + rt[...].reshape(256, 128)).astype(jnp.bfloat16)


def local(amplitudes, integrals):
    out = pl.pallas_call(
        kernel,
        out_shape=jax.ShapeDtypeStruct((256, 128), jnp.bfloat16),
        in_specs=[pl.BlockSpec(memory_space=pl.ANY)] * 2,
        out_specs=pl.BlockSpec(memory_space=pltpu.VMEM),
        scratch_shapes=[
            pltpu.VMEM((4, 4, 2, 64, 384), jnp.bfloat16),
            pltpu.VMEM((2, 2, 2, 4, 64, 384), jnp.bfloat16),
            pltpu.VMEM((4, 4, 256, 256), F32),
            pltpu.VMEM((4, 2, 128, 256), F32),
            pltpu.VMEM((4, 2, 128, 256), F32),
            pltpu.VMEM((4, 2, 128, 256), F32),
            pltpu.VMEM((4, 2, 128, 256), F32),
            pltpu.VMEM((4, 2, 2, 64, 256), F32),
            pltpu.VMEM((4, 2, 64, 256), F32),
            pltpu.VMEM((4, 2, 64, 256), F32),
            pltpu.VMEM((4, 64, 256), F32),
            pltpu.VMEM((2, 2, 64, 256), F32),
            pltpu.VMEM((2, 64, 256), F32),
            pltpu.VMEM((2, 64, 256), F32),
            pltpu.VMEM((2, 64, 256), F32),
            pltpu.VMEM((2, 2, 64, 128), F32),
            pltpu.SemaphoreType.DMA((len(NAMES),)),
            pltpu.SemaphoreType.DMA((len(NAMES),)),
            pltpu.SemaphoreType.DMA((2,)),
        ],
        compiler_params=pltpu.CompilerParams(
            collective_id=0, has_side_effects=True, vmem_limit_bytes=48 * 1024 * 1024
        ),
    )(amplitudes, integrals)
    out = jnp.transpose(out.reshape(4, 64, 2, 64), (0, 2, 1, 3))
    return out.reshape(4, 2, 4096)


def solution(mesh):
    in_specs = (P("ia", "ja", None, None), P("ja", "ia", None, None))
    out_specs = P("ia", "ja", None)
    return jax.shard_map(local, mesh=mesh, in_specs=in_specs, out_specs=out_specs, check_vma=False)
```

```python
import jax
import jax.numpy as jnp
from jax import lax
from jax.experimental import pallas as pl
from jax.experimental.pallas import tpu as pltpu
from jax.sharding import PartitionSpec as P

MESH = pl.DeviceIdType.MESH
F32 = jnp.float32
ROWS = 16
PARTS = 64 // ROWS
STAGES = 2 * PARTS
AHEAD = 4
CAME = (24, 30, 36, 42)
READY = (27, 33, 39, 45)

NAMES = (
    ["a1", "a2", "a3", "w"]
    + [f"{n}{p}" for n in ("cross", "cf") for p in range(PARTS)]
    + [f"{n}{s}" for n in ("m1p", "m1m", "m2p", "m2m", "m3p", "m3m", "z1", "z2") for s in range(STAGES)]
    + [f"{n}{p}" for n in ("z4", "sw") for p in range(PARTS)]
    + [f"t{q}{p}" for p in range(PARTS) for q in range(2)]
)
INDEX = {name: n for n, name in enumerate(NAMES)}


LEVELS = 21
FINE = 10.4 * 256
TINY = 1e-30
CODED = True
WORDS, WORD = (3, jnp.bfloat16) if CODED else (2, jnp.float32)


def remainder(value, rounded):
    return jnp.round((value - rounded) * (FINE * pl.reciprocal(jnp.maximum(jnp.abs(rounded), TINY), approx=True)))


def encode(ref, first, second):
    if not CODED:
        ref[0], ref[1] = first, second
        return
    one, two = first.astype(jnp.bfloat16), second.astype(jnp.bfloat16)
    ref[0], ref[1] = one, two
    rest = remainder(first, one.astype(F32)) * LEVELS + remainder(second, two.astype(F32))
    ref[2] = rest.astype(jnp.bfloat16)


def decode(ref):
    if not CODED:
        return ref[0], ref[1]
    one, two, rest = ref[0].astype(F32), ref[1].astype(F32), ref[2].astype(F32)
    upper = jnp.round(rest * (1 / LEVELS))
    lower = rest - upper * LEVELS
    return one + upper * (jnp.abs(one) * (1 / FINE)), two + lower * (jnp.abs(two) * (1 / FINE))


def plan():
    steps = []
    for p in range(PARTS):
        for at, what in ((20 + 1.2 * p, "product"), (25 + 2.6 * p, "y_pass"), (29 + 2.8 * p, "y_end"),
                         (33 + 3 * p, "z_second"), (37 + 3 * p, "z_third")):
            steps.append((at, what, p))
        came = CAME[p]
        ready = READY[p]
        steps.append((came, "arrive", p))
        for offset, what in ((0, "product"), (5, "y_pass"), (9, "y_end"), (12.5, "z_second"), (16, "z_third")):
            steps.append((ready + offset, what, PARTS + p))
        steps.append((ready + 21, "last", p))
        steps.append((ready + 80, "finish", p))
    return [(what, n) for _, what, n in sorted(steps, key=lambda step: step[0])]


def kernel(a_ref, w_ref, o_ref, abuf, wbuf, t, y_out, y_in, e, z1_out, z1, f, z2_out, z2, g, z4_out, z4, gsum, drecv, rt, ss, rs, ls):
    ia, ja = lax.axis_index("ia"), lax.axis_index("ja")
    x, zh, c = ia // 4, (ia // 2) % 2, ia % 2
    y, zl = ja // 8, ja % 8
    b2, b1, b0 = zl // 4, (zl // 2) % 2, zl % 2
    keep = (b2 + zh) % 2

    def device(x, y, zh, zl, c):
        return (x * 4 + zh * 2 + c, y * 8 + zl)

    y_up, y_down = (y + 1) % 4, (y + 3) % 4

    sibling = device(x, y, zh, zl, 1 - c)
    a_to = [device((x + n) % 4, y, zh, zl, c) for n in (1, 3, 2)]
    anti = device(x, y, 1 - zh, zl, c)
    above, below = device(x, y_up, zh, zl, c), device(x, y_down, zh, zl, c)
    near = device(x, y, zh, b2 * 4 + b1 * 2 + 1 - b0, c)
    next_pair = device(x, y, zh, b2 * 4 + (1 - b1) * 2 + b0, c)
    far = device(x, y, zh, (1 - b2) * 4 + b1 * 2 + b0, c)

    swap = device(y, x, zh, zl, c)
    t_to = [device(x, y, b2, zh * 4 + c * 2 + q, b1) for q in range(2)]
    stays = x == y
    same = jnp.logical_and(b2 == zh, b1 == c)

    barrier = pltpu.get_barrier_semaphore()

    def greet(target):
        pl.semaphore_signal(barrier, inc=1, device_id=target, device_id_type=MESH)

    for target in (sibling, *a_to, anti, above, below, near, next_pair, far):
        greet(target)

    @pl.when(jnp.logical_not(stays))
    def _():
        greet(swap)

    for q in range(2):

        @pl.when(jnp.logical_not(jnp.logical_and(same, b0 == q)))
        def _():
            greet(t_to[q])

    pl.semaphore_wait(barrier, 13 - jnp.where(stays, 1, 0) - jnp.where(same, 1, 0))

    live = {}

    def copy(name, src, dst, target):
        n = INDEX[name]
        return pltpu.make_async_remote_copy(
            src_ref=src, dst_ref=dst, send_sem=ss.at[n], recv_sem=rs.at[n], device_id=target, device_id_type=MESH
        )

    def begin(name, *rest):
        live[name] = copy(name, *rest)
        live[name].start()

    def chunk(p):
        return pl.ds(p * ROWS, ROWS)

    def start_cross(p):
        begin(f"cross{p}", w_ref.at[:, :, chunk(p)], wbuf.at[1, c, :, :, chunk(p)], anti)

    for p in range(min(AHEAD, PARTS)):
        start_cross(p)
    for n in range(3):
        begin(f"a{n + 1}", a_ref, abuf.at[x], a_to[n])
    begin("w", w_ref, wbuf.at[0, c], sibling)
    own_a = pltpu.make_async_copy(a_ref, abuf.at[x], ls.at[0])
    own_w = pltpu.make_async_copy(w_ref, wbuf.at[0, c], ls.at[1])
    own_a.start()
    own_w.start()
    own_a.wait()
    own_w.wait()
    for name in ("w", "a1", "a2", "a3"):
        live[name].wait()

    def arrive(p):
        live[f"cross{p}"].wait()
        if p + AHEAD < PARTS:
            start_cross(p + AHEAD)
        part = wbuf.at[1, c, :, :, chunk(p)]
        begin(f"cf{p}", part, part, sibling)

    half = 4 * ROWS
    low, high = pl.ds(0, half), pl.ds(half, half)

    def product(s):
        sel, p = s // PARTS, s % PARTS
        if sel:
            live[f"cf{p}"].wait()

        def one(n, _):
            total = None
            for k in range(2):
                left = wbuf[sel, :, k, :, chunk(p)].reshape(8 * ROWS, 384)
                right = abuf[n, :, k].reshape(256, 384)
                part = lax.dot_general(left, right, (((1,), (1,)), ((), ())), preferred_element_type=F32)
                total = part if total is None else total + part
            t[s, n] = total
            return 0

        lax.fori_loop(0, 4, one, 0)
        y_send(s, 0, "m1p", t[s, (y + 2) % 4, low], above)
        y_send(s, 1, "m1m", t[s, (y + 2) % 4, high], below)
        y_send(s, 2, "m2p", t[s, y_up, high], above)
        y_send(s, 3, "m2m", t[s, y_down, low], below)

    def y_send(s, n, name, value, target):
        encode(y_out.at[s, n], value[: half // 2], value[half // 2 :])
        begin(f"{name}{s}", y_out.at[s, n], y_in.at[s, n], target)

    def y_got(s, n):
        return jnp.concatenate(decode(y_in.at[s, n]), axis=0)

    def y_pass(s):
        live[f"m1p{s}"].wait()
        y_send(s, 4, "m3p", y_got(s, 0) + t[s, y_up, low], above)
        live[f"m1m{s}"].wait()
        y_send(s, 5, "m3m", y_got(s, 1) + t[s, y_down, high], below)

    def y_end(s):
        for name in ("m2p", "m2m", "m3p", "m3m"):
            live[f"{name}{s}"].wait()
        e[s, 0] = (t[s, y, low] + y_got(s, 4) + y_got(s, 3)).reshape(2, 2 * ROWS, 256)
        e[s, 1] = (t[s, y, high] + y_got(s, 2) + y_got(s, 5)).reshape(2, 2 * ROWS, 256)
        encode(z1_out.at[s], e[s, 0, 1 - b0], e[s, 1, 1 - b0])
        begin(f"z1{s}", z1_out.at[s], z1.at[s], near)

    def z_second(s):
        live[f"z1{s}"].wait()
        got = decode(z1.at[s])
        f[s, 0] = e[s, 0, b0] + got[0]
        f[s, 1] = e[s, 1, b0] + got[1]
        encode(z2_out.at[s], f[s, 1 - b1, :ROWS], f[s, 1 - b1, ROWS:])
        begin(f"z2{s}", z2_out.at[s], z2.at[s], next_pair)

    def z_third(s):
        sel, p = s // PARTS, s % PARTS
        live[f"z2{s}"].wait()
        g[p, sel] = f[s, b1].reshape(2, ROWS, 256)
        got = decode(z2.at[s])
        g[p, sel, 0] += got[0]
        g[p, sel, 1] += got[1]

        @pl.when(keep != sel)
        def _():
            encode(z4_out.at[p], g[p, sel, 0], g[p, sel, 1])
            copy(f"z4{p}", z4_out.at[p], z4.at[p], far).start()

    def swapped(p):
        return copy(f"sw{p}", gsum.at[p], drecv.at[:, chunk(p)], swap)

    def last(p):
        copy(f"z4{p}", z4_out.at[p], z4.at[p], far).wait()
        got = decode(z4.at[p])
        gsum[p, 0] = g[p, keep, 0] + got[0]
        gsum[p, 1] = g[p, keep, 1] + got[1]

        @pl.when(stays)
        def _():
            drecv[:, chunk(p)] = gsum[p]

        @pl.when(jnp.logical_not(stays))
        def _():
            swapped(p).start()

        for q in range(2):
            itself = jnp.logical_and(same, b0 == q)

            @pl.when(itself)
            def _():
                rt[b0, :, chunk(p)] = gsum[p, :, :, q * 128 : (q + 1) * 128]

            @pl.when(jnp.logical_not(itself))
            def _():
                pltpu.make_async_remote_copy(
                    src_ref=gsum.at[p, :, :, pl.ds(q * 128, 128)],
                    dst_ref=rt.at[b0, :, chunk(p)],
                    send_sem=ss.at[INDEX[f"t{q}{p}"]],
                    recv_sem=rs.at[INDEX[f"t0{p}"] + b0],
                    device_id=t_to[q],
                    device_id_type=MESH,
                ).start()

    def finish(p):
        @pl.when(jnp.logical_not(stays))
        def _():
            swapped(p).wait()

        for q in range(2):

            @pl.when(jnp.logical_not(jnp.logical_and(same, b0 == q)))
            def _():
                copy(f"t{q}{p}", gsum.at[p, :, :, pl.ds(q * 128, 128)], rt.at[q, :, chunk(p)], t_to[q]).wait()

    what = dict(
        arrive=arrive, product=product, y_pass=y_pass, y_end=y_end, z_second=z_second, z_third=z_third,
        last=last, finish=finish,
    )
    for name, n in plan():
        what[name](n)
    d = jnp.transpose(drecv[...].reshape(128, 256))
    o_ref[...] = (d + rt[...].reshape(256, 128)).astype(jnp.bfloat16)


def local(amplitudes, integrals):
    out = pl.pallas_call(
        kernel,
        out_shape=jax.ShapeDtypeStruct((256, 128), jnp.bfloat16),
        in_specs=[pl.BlockSpec(memory_space=pltpu.HBM)] * 2,
        out_specs=pl.BlockSpec(memory_space=pltpu.VMEM),
        scratch_shapes=[
            pltpu.VMEM((4, 4, 2, 64, 384), jnp.bfloat16),
            pltpu.VMEM((2, 2, 2, 4, 64, 384), jnp.bfloat16),
            pltpu.VMEM((STAGES, 4, 8 * ROWS, 256), F32),
            pltpu.VMEM((STAGES, 6, WORDS, 2 * ROWS, 256), WORD),
            pltpu.VMEM((STAGES, 6, WORDS, 2 * ROWS, 256), WORD),
            pltpu.VMEM((STAGES, 2, 2, 2 * ROWS, 256), F32),
            pltpu.VMEM((STAGES, WORDS, 2 * ROWS, 256), WORD),
            pltpu.VMEM((STAGES, WORDS, 2 * ROWS, 256), WORD),
            pltpu.VMEM((STAGES, 2, 2 * ROWS, 256), F32),
            pltpu.VMEM((STAGES, WORDS, ROWS, 256), WORD),
            pltpu.VMEM((STAGES, WORDS, ROWS, 256), WORD),
            pltpu.VMEM((PARTS, 2, 2, ROWS, 256), F32),
            pltpu.VMEM((PARTS, WORDS, ROWS, 256), WORD),
            pltpu.VMEM((PARTS, WORDS, ROWS, 256), WORD),
            pltpu.VMEM((PARTS, 2, ROWS, 256), F32),
            pltpu.VMEM((2, 64, 256), F32),
            pltpu.VMEM((2, 2, 64, 128), F32),
            pltpu.SemaphoreType.DMA((len(NAMES),)),
            pltpu.SemaphoreType.DMA((len(NAMES),)),
            pltpu.SemaphoreType.DMA((2,)),
        ],
        compiler_params=pltpu.CompilerParams(
            collective_id=0, has_side_effects=True, vmem_limit_bytes=48 * 1024 * 1024
        ),
    )(amplitudes, integrals)
    out = jnp.transpose(out.reshape(4, 64, 2, 64), (0, 2, 1, 3))
    return out.reshape(4, 2, 4096)


def solution(mesh):
    in_specs = (P("ia", "ja", None, None), P("ja", "ia", None, None))
    out_specs = P("ia", "ja", None)
    return jax.shard_map(local, mesh=mesh, in_specs=in_specs, out_specs=out_specs, check_vma=False)
```

```python
import jax
import jax.numpy as jnp
from jax import lax
from jax.experimental import pallas as pl
from jax.experimental.pallas import tpu as pltpu
from jax.sharding import PartitionSpec as P

MESH = pl.DeviceIdType.MESH
F32 = jnp.float32
ROWS = 16
PARTS = 64 // ROWS
STAGES = 2 * PARTS
DIRECT = (6, 7)
AHEAD = 4
CAME = (22, 28, 34, 40)

NAMES = (
    ["a1", "a2", "a3", "w"]
    + [f"{n}{p}" for n in ("cross", "cf") for p in range(PARTS)]
    + [f"{n}{s}" for n in ("y0", "y1", "y2", "y3", "y4", "y5", "z1", "z2", "z3") for s in range(STAGES)]
    + [f"{n}{p}" for n in ("z4", "sw") for p in range(PARTS)]
    + [f"t{q}{p}" for p in range(PARTS) for q in range(2)]
)
INDEX = {name: n for n, name in enumerate(NAMES)}


LEVELS = 21
FINE = 10.4 * 256
TINY = 1e-30
CODED = True
WORDS, WORD = (3, jnp.bfloat16) if CODED else (2, jnp.float32)


def remainder(value, rounded):
    return jnp.round((value - rounded) * (FINE * pl.reciprocal(jnp.maximum(jnp.abs(rounded), TINY), approx=True)))


def encode(ref, first, second):
    if not CODED:
        ref[0], ref[1] = first, second
        return
    one, two = first.astype(jnp.bfloat16), second.astype(jnp.bfloat16)
    ref[0], ref[1] = one, two
    rest = remainder(first, one.astype(F32)) * LEVELS + remainder(second, two.astype(F32))
    ref[2] = rest.astype(jnp.bfloat16)


def decode(ref):
    if not CODED:
        return ref[0], ref[1]
    one, two, rest = ref[0].astype(F32), ref[1].astype(F32), ref[2].astype(F32)
    upper = jnp.round(rest * (1 / LEVELS))
    lower = rest - upper * LEVELS
    return one + upper * (jnp.abs(one) * (1 / FINE)), two + lower * (jnp.abs(two) * (1 / FINE))


def plan():
    steps = []
    for p in range(PARTS):
        for at, what in ((20 + 1.2 * p, "product"), (26 + 3.5 * p, "y_pass"), (32 + 3.5 * p, "y_end"), (37 + 3.5 * p, "z_end")):
            steps.append((at, what, p))
        steps.append((CAME[p], "arrive", p))
        ready, offsets = CAME[p] + 3, (5, 9, 17) if PARTS + p in DIRECT else (9, 13, 21)
        steps.append((ready, "product", PARTS + p))
        steps.append((ready + 5.05, "y_pass", PARTS + p))
        steps.append((ready + offsets[0], "y_end", PARTS + p))
        steps.append((ready + offsets[1], "z_end", PARTS + p))
        steps.append((max(ready + offsets[2], 37.1 + 3.5 * p), "last", p))
        steps.append((ready + 100, "finish", p))
    return [(what, n) for _, what, n in sorted(steps, key=lambda step: step[0])]


def kernel(a_ref, w_ref, o_ref, abuf, wbuf, t, y_out, y_in, e, z_out, z_in, g, z4_out, z4, gsum, drecv, rt, ss, rs, ls):
    ia, ja = lax.axis_index("ia"), lax.axis_index("ja")
    x, zh, c = ia // 4, (ia // 2) % 2, ia % 2
    y, zl = ja // 8, ja % 8
    b2, b1, b0 = zl // 4, (zl // 2) % 2, zl % 2
    keep = (b2 + zh) % 2

    def device(x, y, zh, zl, c):
        return (x * 4 + zh * 2 + c, y * 8 + zl)


    sibling = device(x, y, zh, zl, 1 - c)
    a_to = [device((x + n) % 4, y, zh, zl, c) for n in (1, 3, 2)]
    anti = device(x, y, 1 - zh, zl, c)
    y_to = [device(x, (y + n) % 4, zh, zl, c) for n in range(4)]
    quad = [(b1, b0), (b1, 1 - b0), (1 - b1, b0), (1 - b1, 1 - b0)]
    z_to = [device(x, y, zh, b2 * 4 + two * 2 + one, c) for two, one in quad]
    far = device(x, y, zh, (1 - b2) * 4 + b1 * 2 + b0, c)

    swap = device(y, x, zh, zl, c)
    t_to = [device(x, y, b2, zh * 4 + c * 2 + q, b1) for q in range(2)]
    stays = x == y
    same = jnp.logical_and(b2 == zh, b1 == c)

    barrier = pltpu.get_barrier_semaphore()

    def greet(target):
        pl.semaphore_signal(barrier, inc=1, device_id=target, device_id_type=MESH)

    for target in (sibling, anti, far, *a_to, *y_to[1:], *z_to[1:]):
        greet(target)

    @pl.when(jnp.logical_not(stays))
    def _():
        greet(swap)

    for q in range(2):

        @pl.when(jnp.logical_not(jnp.logical_and(same, b0 == q)))
        def _():
            greet(t_to[q])

    pl.semaphore_wait(barrier, 15 - jnp.where(stays, 1, 0) - jnp.where(same, 1, 0))

    live = {}

    def copy(name, src, dst, target):
        n = INDEX[name]
        return pltpu.make_async_remote_copy(
            src_ref=src, dst_ref=dst, send_sem=ss.at[n], recv_sem=rs.at[n], device_id=target, device_id_type=MESH
        )

    def begin(name, *rest):
        live[name] = copy(name, *rest)
        live[name].start()

    def chunk(p):
        return pl.ds(p * ROWS, ROWS)

    def start_cross(p):
        begin(f"cross{p}", w_ref.at[:, :, chunk(p)], wbuf.at[1, c, :, :, chunk(p)], anti)

    for p in range(min(AHEAD, PARTS)):
        start_cross(p)
    for n in range(3):
        begin(f"a{n + 1}", a_ref, abuf.at[x], a_to[n])
    begin("w", w_ref, wbuf.at[0, c], sibling)
    own_a = pltpu.make_async_copy(a_ref, abuf.at[x], ls.at[0])
    own_w = pltpu.make_async_copy(w_ref, wbuf.at[0, c], ls.at[1])
    own_a.start()
    own_w.start()
    own_a.wait()
    own_w.wait()
    for name in ("w", "a1", "a2", "a3"):
        live[name].wait()

    def arrive(p):
        live[f"cross{p}"].wait()
        if p + AHEAD < PARTS:
            start_cross(p + AHEAD)
        part = wbuf.at[1, c, :, :, chunk(p)]
        begin(f"cf{p}", part, part, sibling)

    low, high = pl.ds(0, 4 * ROWS), pl.ds(4 * ROWS, 4 * ROWS)

    def product(s):
        sel, p = s // PARTS, s % PARTS
        if sel:
            live[f"cf{p}"].wait()

        def one(n, _):
            total = None
            for k in range(2):
                left = wbuf[sel, :, k, :, chunk(p)].reshape(8 * ROWS, 384)
                right = abuf[n, :, k].reshape(256, 384)
                part = lax.dot_general(left, right, (((1,), (1,)), ((), ())), preferred_element_type=F32)
                total = part if total is None else total + part
            t[s, n] = total
            return 0

        lax.fori_loop(0, 4, one, 0)
        direct = s in DIRECT
        y_send(s, 0, t[s, (y + 2) % 4, low], y_to[2 if direct else 1])
        y_send(s, 1, t[s, (y + 2) % 4, high], y_to[2 if direct else 3])
        y_send(s, 2, t[s, (y + 1) % 4, high], y_to[1])
        y_send(s, 3, t[s, (y + 3) % 4, low], y_to[3])
        if direct:
            y_send(s, 4, t[s, (y + 1) % 4, low], y_to[1])
            y_send(s, 5, t[s, (y + 3) % 4, high], y_to[3])

    def y_send(s, n, value, target):
        encode(y_out.at[s, n], value[: 2 * ROWS], value[2 * ROWS :])
        begin(f"y{n}{s}", y_out.at[s, n], y_in.at[s, n], target)

    def y_got(s, n):
        live[f"y{n}{s}"].wait()
        return jnp.concatenate(decode(y_in.at[s, n]), axis=0)

    def y_pass(s):
        if s not in DIRECT:
            y_send(s, 4, y_got(s, 0) + t[s, (y + 1) % 4, low], y_to[1])
            y_send(s, 5, y_got(s, 1) + t[s, (y + 3) % 4, high], y_to[3])

    def y_end(s):
        first = t[s, y, low] + y_got(s, 3)
        second = t[s, y, high] + y_got(s, 2)
        if s in DIRECT:
            first += y_got(s, 0)
            second += y_got(s, 1)
        first += y_got(s, 4)
        second += y_got(s, 5)
        e[s, 0] = first.reshape(2, 2, ROWS, 256)
        e[s, 1] = second.reshape(2, 2, ROWS, 256)
        for n in (3, 2, 1):
            two, one = quad[n]
            encode(z_out.at[s, n - 1], e[s, two, one, 0], e[s, two, one, 1])
            begin(f"z{n}{s}", z_out.at[s, n - 1], z_in.at[s, n - 1], z_to[n])

    def z_end(s):
        sel, p = s // PARTS, s % PARTS
        first, second = e[s, b1, b0, 0], e[s, b1, b0, 1]
        for n in (1, 2, 3):
            live[f"z{n}{s}"].wait()
            got = decode(z_in.at[s, n - 1])
            first, second = first + got[0], second + got[1]
        g[p, sel, 0] = first
        g[p, sel, 1] = second

        @pl.when(keep != sel)
        def _():
            encode(z4_out.at[p], g[p, sel, 0], g[p, sel, 1])
            copy(f"z4{p}", z4_out.at[p], z4.at[p], far).start()

    def swapped(p):
        return copy(f"sw{p}", gsum.at[p], drecv.at[:, chunk(p)], swap)

    def last(p):
        copy(f"z4{p}", z4_out.at[p], z4.at[p], far).wait()
        got = decode(z4.at[p])
        gsum[p, 0] = g[p, keep, 0] + got[0]
        gsum[p, 1] = g[p, keep, 1] + got[1]

        @pl.when(stays)
        def _():
            drecv[:, chunk(p)] = gsum[p]

        @pl.when(jnp.logical_not(stays))
        def _():
            swapped(p).start()

        for q in range(2):
            itself = jnp.logical_and(same, b0 == q)

            @pl.when(itself)
            def _():
                rt[b0, :, chunk(p)] = gsum[p, :, :, q * 128 : (q + 1) * 128]

            @pl.when(jnp.logical_not(itself))
            def _():
                pltpu.make_async_remote_copy(
                    src_ref=gsum.at[p, :, :, pl.ds(q * 128, 128)],
                    dst_ref=rt.at[b0, :, chunk(p)],
                    send_sem=ss.at[INDEX[f"t{q}{p}"]],
                    recv_sem=rs.at[INDEX[f"t0{p}"] + b0],
                    device_id=t_to[q],
                    device_id_type=MESH,
                ).start()

    def finish(p):
        @pl.when(jnp.logical_not(stays))
        def _():
            swapped(p).wait()

        for q in range(2):

            @pl.when(jnp.logical_not(jnp.logical_and(same, b0 == q)))
            def _():
                copy(f"t{q}{p}", gsum.at[p, :, :, pl.ds(q * 128, 128)], rt.at[q, :, chunk(p)], t_to[q]).wait()

    what = dict(arrive=arrive, product=product, y_pass=y_pass, y_end=y_end, z_end=z_end, last=last, finish=finish)
    for name, n in plan():
        what[name](n)
    d = jnp.transpose(drecv[...].reshape(128, 256))
    o_ref[...] = (d + rt[...].reshape(256, 128)).astype(jnp.bfloat16)


def local(amplitudes, integrals):
    out = pl.pallas_call(
        kernel,
        out_shape=jax.ShapeDtypeStruct((256, 128), jnp.bfloat16),
        in_specs=[pl.BlockSpec(memory_space=pltpu.HBM)] * 2,
        out_specs=pl.BlockSpec(memory_space=pltpu.VMEM),
        scratch_shapes=[
            pltpu.VMEM((4, 4, 2, 64, 384), jnp.bfloat16),
            pltpu.VMEM((2, 2, 2, 4, 64, 384), jnp.bfloat16),
            pltpu.VMEM((STAGES, 4, 8 * ROWS, 256), F32),
            pltpu.VMEM((STAGES, 6, WORDS, 2 * ROWS, 256), WORD),
            pltpu.VMEM((STAGES, 6, WORDS, 2 * ROWS, 256), WORD),
            pltpu.VMEM((STAGES, 2, 2, 2, ROWS, 256), F32),
            pltpu.VMEM((STAGES, 3, WORDS, ROWS, 256), WORD),
            pltpu.VMEM((STAGES, 3, WORDS, ROWS, 256), WORD),
            pltpu.VMEM((PARTS, 2, 2, ROWS, 256), F32),
            pltpu.VMEM((PARTS, WORDS, ROWS, 256), WORD),
            pltpu.VMEM((PARTS, WORDS, ROWS, 256), WORD),
            pltpu.VMEM((PARTS, 2, ROWS, 256), F32),
            pltpu.VMEM((2, 64, 256), F32),
            pltpu.VMEM((2, 2, 64, 128), F32),
            pltpu.SemaphoreType.DMA((len(NAMES),)),
            pltpu.SemaphoreType.DMA((len(NAMES),)),
            pltpu.SemaphoreType.DMA((2,)),
        ],
        compiler_params=pltpu.CompilerParams(
            collective_id=0, has_side_effects=True, vmem_limit_bytes=48 * 1024 * 1024
        ),
    )(amplitudes, integrals)
    out = jnp.transpose(out.reshape(4, 64, 2, 64), (0, 2, 1, 3))
    return out.reshape(4, 2, 4096)


def solution(mesh):
    in_specs = (P("ia", "ja", None, None), P("ja", "ia", None, None))
    out_specs = P("ia", "ja", None)
    return jax.shard_map(local, mesh=mesh, in_specs=in_specs, out_specs=out_specs, check_vma=False)
```

```python
import jax
import jax.numpy as jnp
from jax import lax
from jax.experimental import pallas as pl
from jax.experimental.pallas import tpu as pltpu
from jax.sharding import PartitionSpec as P

MESH = pl.DeviceIdType.MESH
F32 = jnp.float32
ROWS = 16
PARTS = 64 // ROWS
STAGES = 2 * PARTS
DIRECT = (6, 7)
AHEAD = 4
CAME = (22, 28, 34, 40)

NAMES = (
    ["a1", "a2", "a3", "w"]
    + [f"{n}{p}" for n in ("cross", "cf") for p in range(PARTS)]
    + [f"{n}{s}" for n in ("y0", "y1", "y2", "y3", "y4", "y5", "z1", "z2", "z3") for s in range(STAGES)]
    + [f"{n}{p}" for n in ("z4", "sw") for p in range(PARTS)]
    + [f"t{q}{p}" for p in range(PARTS) for q in range(2)]
)
INDEX = {name: n for n, name in enumerate(NAMES)}


LEVELS = 21
FINE = 10.4 * 256
TINY = 1e-30
CODED = True
WORDS, WORD = (3, jnp.bfloat16) if CODED else (2, jnp.float32)


def remainder(value, rounded):
    return jnp.round((value - rounded) * (FINE * pl.reciprocal(jnp.maximum(jnp.abs(rounded), TINY), approx=True)))


def encode(ref, first, second):
    if not CODED:
        ref[0], ref[1] = first, second
        return
    one, two = first.astype(jnp.bfloat16), second.astype(jnp.bfloat16)
    ref[0], ref[1] = one, two
    rest = remainder(first, one.astype(F32)) * LEVELS + remainder(second, two.astype(F32))
    ref[2] = rest.astype(jnp.bfloat16)


def decode(ref):
    if not CODED:
        return ref[0], ref[1]
    one, two, rest = ref[0].astype(F32), ref[1].astype(F32), ref[2].astype(F32)
    upper = jnp.round(rest * (1 / LEVELS))
    lower = rest - upper * LEVELS
    return one + upper * (jnp.abs(one) * (1 / FINE)), two + lower * (jnp.abs(two) * (1 / FINE))


def plan():
    steps = []
    for p in range(PARTS):
        for at, what in ((20 + 1.2 * p, "product"), (26 + 3.5 * p, "y_pass"), (32 + 3.5 * p, "y_end"), (37 + 3.5 * p, "z_end")):
            steps.append((at, what, p))
        steps.append((CAME[p], "arrive", p))
        ready, offsets = CAME[p] + 3, (5, 9, 17) if PARTS + p in DIRECT else (9, 13, 21)
        steps.append((ready, "product", PARTS + p))
        steps.append((ready + 5.05, "y_pass", PARTS + p))
        steps.append((ready + offsets[0], "y_end", PARTS + p))
        steps.append((ready + offsets[1], "z_end", PARTS + p))
        steps.append((max(ready + offsets[2], 37.1 + 3.5 * p), "last", p))
        steps.append((ready + 100, "finish", p))
    return [(what, n) for _, what, n in sorted(steps, key=lambda step: step[0])]


def kernel(a_ref, w_ref, o_ref, abuf, wbuf, t, y_out, y_in, e, z_out, z_in, g, z4_out, z4, gsum, out, d_in, rt_in, drecv, rt, ss, rs, ls):
    ia, ja = lax.axis_index("ia"), lax.axis_index("ja")
    x, zh, c = ia // 4, (ia // 2) % 2, ia % 2
    y, zl = ja // 8, ja % 8
    b2, b1, b0 = zl // 4, (zl // 2) % 2, zl % 2
    keep = (b2 + zh) % 2

    def device(x, y, zh, zl, c):
        return (x * 4 + zh * 2 + c, y * 8 + zl)


    sibling = device(x, y, zh, zl, 1 - c)
    a_to = [device((x + n) % 4, y, zh, zl, c) for n in (1, 3, 2)]
    anti = device(x, y, 1 - zh, zl, c)
    y_to = [device(x, (y + n) % 4, zh, zl, c) for n in range(4)]
    quad = [(b1, b0), (b1, 1 - b0), (1 - b1, b0), (1 - b1, 1 - b0)]
    z_to = [device(x, y, zh, b2 * 4 + two * 2 + one, c) for two, one in quad]
    far = device(x, y, zh, (1 - b2) * 4 + b1 * 2 + b0, c)

    swap = device(y, x, zh, zl, c)
    t_to = [device(x, y, b2, zh * 4 + c * 2 + q, b1) for q in range(2)]
    stays = x == y
    same = jnp.logical_and(b2 == zh, b1 == c)

    barrier = pltpu.get_barrier_semaphore()

    def greet(target):
        pl.semaphore_signal(barrier, inc=1, device_id=target, device_id_type=MESH)

    for target in (sibling, anti, far, *a_to, *y_to[1:], *z_to[1:]):
        greet(target)

    @pl.when(jnp.logical_not(stays))
    def _():
        greet(swap)

    for q in range(2):

        @pl.when(jnp.logical_not(jnp.logical_and(same, b0 == q)))
        def _():
            greet(t_to[q])

    pl.semaphore_wait(barrier, 15 - jnp.where(stays, 1, 0) - jnp.where(same, 1, 0))

    live = {}

    def copy(name, src, dst, target):
        n = INDEX[name]
        return pltpu.make_async_remote_copy(
            src_ref=src, dst_ref=dst, send_sem=ss.at[n], recv_sem=rs.at[n], device_id=target, device_id_type=MESH
        )

    def begin(name, *rest):
        live[name] = copy(name, *rest)
        live[name].start()

    def chunk(p):
        return pl.ds(p * ROWS, ROWS)

    def start_cross(p):
        begin(f"cross{p}", w_ref.at[:, :, chunk(p)], wbuf.at[1, c, :, :, chunk(p)], anti)

    for p in range(min(AHEAD, PARTS)):
        start_cross(p)
    for n in range(3):
        begin(f"a{n + 1}", a_ref, abuf.at[x], a_to[n])
    begin("w", w_ref, wbuf.at[0, c], sibling)
    own_a = pltpu.make_async_copy(a_ref, abuf.at[x], ls.at[0])
    own_w = pltpu.make_async_copy(w_ref, wbuf.at[0, c], ls.at[1])
    own_a.start()
    own_w.start()
    own_a.wait()
    own_w.wait()
    for name in ("w", "a1", "a2", "a3"):
        live[name].wait()

    def arrive(p):
        live[f"cross{p}"].wait()
        if p + AHEAD < PARTS:
            start_cross(p + AHEAD)
        part = wbuf.at[1, c, :, :, chunk(p)]
        begin(f"cf{p}", part, part, sibling)

    low, high = pl.ds(0, 4 * ROWS), pl.ds(4 * ROWS, 4 * ROWS)

    def product(s):
        sel, p = s // PARTS, s % PARTS
        if sel:
            live[f"cf{p}"].wait()

        def one(n, _):
            total = None
            for k in range(2):
                left = wbuf[sel, :, k, :, chunk(p)].reshape(8 * ROWS, 384)
                right = abuf[n, :, k].reshape(256, 384)
                part = lax.dot_general(left, right, (((1,), (1,)), ((), ())), preferred_element_type=F32)
                total = part if total is None else total + part
            t[s, n] = total
            return 0

        lax.fori_loop(0, 4, one, 0)
        direct = s in DIRECT
        y_send(s, 0, t[s, (y + 2) % 4, low], y_to[2 if direct else 1])
        y_send(s, 1, t[s, (y + 2) % 4, high], y_to[2 if direct else 3])
        y_send(s, 2, t[s, (y + 1) % 4, high], y_to[1])
        y_send(s, 3, t[s, (y + 3) % 4, low], y_to[3])
        if direct:
            y_send(s, 4, t[s, (y + 1) % 4, low], y_to[1])
            y_send(s, 5, t[s, (y + 3) % 4, high], y_to[3])

    def y_send(s, n, value, target):
        encode(y_out.at[s, n], value[: 2 * ROWS], value[2 * ROWS :])
        begin(f"y{n}{s}", y_out.at[s, n], y_in.at[s, n], target)

    def y_got(s, n):
        live[f"y{n}{s}"].wait()
        return jnp.concatenate(decode(y_in.at[s, n]), axis=0)

    def y_pass(s):
        if s not in DIRECT:
            y_send(s, 4, y_got(s, 0) + t[s, (y + 1) % 4, low], y_to[1])
            y_send(s, 5, y_got(s, 1) + t[s, (y + 3) % 4, high], y_to[3])

    def y_end(s):
        first = t[s, y, low] + y_got(s, 3)
        second = t[s, y, high] + y_got(s, 2)
        if s in DIRECT:
            first += y_got(s, 0)
            second += y_got(s, 1)
        first += y_got(s, 4)
        second += y_got(s, 5)
        e[s, 0] = first.reshape(2, 2, ROWS, 256)
        e[s, 1] = second.reshape(2, 2, ROWS, 256)
        for n in (3, 2, 1):
            two, one = quad[n]
            encode(z_out.at[s, n - 1], e[s, two, one, 0], e[s, two, one, 1])
            begin(f"z{n}{s}", z_out.at[s, n - 1], z_in.at[s, n - 1], z_to[n])

    def z_end(s):
        sel, p = s // PARTS, s % PARTS
        first, second = e[s, b1, b0, 0], e[s, b1, b0, 1]
        for n in (1, 2, 3):
            live[f"z{n}{s}"].wait()
            got = decode(z_in.at[s, n - 1])
            first, second = first + got[0], second + got[1]
        g[p, sel, 0] = first
        g[p, sel, 1] = second

        @pl.when(keep != sel)
        def _():
            encode(z4_out.at[p], g[p, sel, 0], g[p, sel, 1])
            copy(f"z4{p}", z4_out.at[p], z4.at[p], far).start()

    def swapped(p):
        return copy(f"sw{p}", out.at[p], d_in.at[p], swap)

    def last(p):
        copy(f"z4{p}", z4_out.at[p], z4.at[p], far).wait()
        got = decode(z4.at[p])
        gsum[p, 0] = g[p, keep, 0] + got[0]
        gsum[p, 1] = g[p, keep, 1] + got[1]

        encode(out.at[p], gsum[p, 0], gsum[p, 1])

        @pl.when(stays)
        def _():
            drecv[:, chunk(p)] = gsum[p]

        @pl.when(jnp.logical_not(stays))
        def _():
            swapped(p).start()

        for q in range(2):
            itself = jnp.logical_and(same, b0 == q)

            @pl.when(itself)
            def _():
                rt[b0, :, chunk(p)] = gsum[p, :, :, q * 128 : (q + 1) * 128]

            @pl.when(jnp.logical_not(itself))
            def _():
                pltpu.make_async_remote_copy(
                    src_ref=out.at[p, :, :, pl.ds(q * 128, 128)],
                    dst_ref=rt_in.at[b0, p],
                    send_sem=ss.at[INDEX[f"t{q}{p}"]],
                    recv_sem=rs.at[INDEX[f"t0{p}"] + b0],
                    device_id=t_to[q],
                    device_id_type=MESH,
                ).start()

    def finish(p):
        @pl.when(jnp.logical_not(stays))
        def _():
            swapped(p).wait()
            drecv[0, chunk(p)], drecv[1, chunk(p)] = decode(d_in.at[p])

        for q in range(2):

            @pl.when(jnp.logical_not(jnp.logical_and(same, b0 == q)))
            def _():
                copy(f"t{q}{p}", out.at[p, :, :, pl.ds(q * 128, 128)], rt_in.at[q, p], t_to[q]).wait()
                rt[q, 0, chunk(p)], rt[q, 1, chunk(p)] = decode(rt_in.at[q, p])

    what = dict(arrive=arrive, product=product, y_pass=y_pass, y_end=y_end, z_end=z_end, last=last, finish=finish)
    for name, n in plan():
        what[name](n)
    d = jnp.transpose(drecv[...].reshape(128, 256))
    o_ref[...] = (d + rt[...].reshape(256, 128)).astype(jnp.bfloat16)


def local(amplitudes, integrals):
    out = pl.pallas_call(
        kernel,
        out_shape=jax.ShapeDtypeStruct((256, 128), jnp.bfloat16),
        in_specs=[pl.BlockSpec(memory_space=pltpu.HBM)] * 2,
        out_specs=pl.BlockSpec(memory_space=pltpu.VMEM),
        scratch_shapes=[
            pltpu.VMEM((4, 4, 2, 64, 384), jnp.bfloat16),
            pltpu.VMEM((2, 2, 2, 4, 64, 384), jnp.bfloat16),
            pltpu.VMEM((STAGES, 4, 8 * ROWS, 256), F32),
            pltpu.VMEM((STAGES, 6, WORDS, 2 * ROWS, 256), WORD),
            pltpu.VMEM((STAGES, 6, WORDS, 2 * ROWS, 256), WORD),
            pltpu.VMEM((STAGES, 2, 2, 2, ROWS, 256), F32),
            pltpu.VMEM((STAGES, 3, WORDS, ROWS, 256), WORD),
            pltpu.VMEM((STAGES, 3, WORDS, ROWS, 256), WORD),
            pltpu.VMEM((PARTS, 2, 2, ROWS, 256), F32),
            pltpu.VMEM((PARTS, WORDS, ROWS, 256), WORD),
            pltpu.VMEM((PARTS, WORDS, ROWS, 256), WORD),
            pltpu.VMEM((PARTS, 2, ROWS, 256), F32),
            pltpu.VMEM((PARTS, WORDS, ROWS, 256), WORD),
            pltpu.VMEM((PARTS, WORDS, ROWS, 256), WORD),
            pltpu.VMEM((2, PARTS, WORDS, ROWS, 128), WORD),
            pltpu.VMEM((2, 64, 256), F32),
            pltpu.VMEM((2, 2, 64, 128), F32),
            pltpu.SemaphoreType.DMA((len(NAMES),)),
            pltpu.SemaphoreType.DMA((len(NAMES),)),
            pltpu.SemaphoreType.DMA((2,)),
        ],
        compiler_params=pltpu.CompilerParams(
            collective_id=0, has_side_effects=True, vmem_limit_bytes=48 * 1024 * 1024
        ),
    )(amplitudes, integrals)
    out = jnp.transpose(out.reshape(4, 64, 2, 64), (0, 2, 1, 3))
    return out.reshape(4, 2, 4096)


def solution(mesh):
    in_specs = (P("ia", "ja", None, None), P("ja", "ia", None, None))
    out_specs = P("ia", "ja", None)
    return jax.shard_map(local, mesh=mesh, in_specs=in_specs, out_specs=out_specs, check_vma=False)
```

```python
import jax
import jax.numpy as jnp
from jax import lax
from jax.experimental import pallas as pl
from jax.experimental.pallas import tpu as pltpu
from jax.sharding import PartitionSpec as P

MESH = pl.DeviceIdType.MESH
F32 = jnp.float32
ROWS = 16
PARTS = 64 // ROWS
STAGES = 2 * PARTS
DIRECT = (6, 7)
AHEAD = 4
CAME = (22, 28, 34, 40)

NAMES = (
    ["a1", "a2", "a3", "w"]
    + [f"{n}{p}" for n in ("cross", "cf") for p in range(PARTS)]
    + [f"{n}{s}" for n in ("y0", "y1", "y2", "y3", "y4", "y5", "z1", "z2", "z3") for s in range(STAGES)]
    + [f"{n}{p}" for n in ("z4", "sw") for p in range(PARTS)]
    + [f"t{q}{p}" for p in range(PARTS) for q in range(2)]
)
INDEX = {name: n for n, name in enumerate(NAMES)}


LEVELS = 21
FINE = 10.4 * 256
TINY = 1e-30
CODED = True
WORDS, WORD = (3, jnp.bfloat16) if CODED else (2, jnp.float32)


def remainder(value, rounded):
    return jnp.round((value - rounded) * (FINE * pl.reciprocal(jnp.maximum(jnp.abs(rounded), TINY), approx=True)))


def encode(ref, first, second):
    if not CODED:
        ref[0], ref[1] = first, second
        return
    one, two = first.astype(jnp.bfloat16), second.astype(jnp.bfloat16)
    ref[0], ref[1] = one, two
    rest = remainder(first, one.astype(F32)) * LEVELS + remainder(second, two.astype(F32))
    ref[2] = rest.astype(jnp.bfloat16)


def decode(ref):
    if not CODED:
        return ref[0], ref[1]
    one, two, rest = ref[0].astype(F32), ref[1].astype(F32), ref[2].astype(F32)
    upper = jnp.round(rest * (1 / LEVELS))
    lower = rest - upper * LEVELS
    return one + upper * (jnp.abs(one) * (1 / FINE)), two + lower * (jnp.abs(two) * (1 / FINE))


def plan():
    steps = []
    for p in range(PARTS):
        for at, what in ((20 + 1.2 * p, "product"), (26 + 3.5 * p, "y_pass"), (32 + 3.5 * p, "y_end"), (37 + 3.5 * p, "z_end")):
            steps.append((at, what, p))
        steps.append((CAME[p], "arrive", p))
        ready, offsets = CAME[p] + 3, (5, 9, 17) if PARTS + p in DIRECT else (9, 13, 21)
        steps.append((ready, "product", PARTS + p))
        steps.append((ready + 5.05, "y_pass", PARTS + p))
        steps.append((ready + offsets[0], "y_end", PARTS + p))
        steps.append((ready + offsets[1], "z_end", PARTS + p))
        steps.append((max(ready + offsets[2], 37.1 + 3.5 * p), "last", p))
        steps.append((ready + 100, "finish", p))
    return [(what, n) for _, what, n in sorted(steps, key=lambda step: step[0])]


def kernel(a_ref, w_ref, o_ref, abuf, wbuf, t, y_out, y_in, e, z_out, z_in, g, z4_out, z4, gsum, drecv, rt, ss, rs, ls):
    ia, ja = lax.axis_index("ia"), lax.axis_index("ja")
    x, zh, c = ia // 4, (ia // 2) % 2, ia % 2
    y, zl = ja // 8, ja % 8
    b2, b1, b0 = zl // 4, (zl // 2) % 2, zl % 2
    keep = (b2 + zh) % 2

    def device(x, y, zh, zl, c):
        return (x * 4 + zh * 2 + c, y * 8 + zl)


    sibling = device(x, y, zh, zl, 1 - c)
    a_to = [device((x + n) % 4, y, zh, zl, c) for n in (1, 3, 2)]
    anti = device(x, y, 1 - zh, zl, c)
    y_to = [device(x, (y + n) % 4, zh, zl, c) for n in range(4)]
    quad = [(b1, b0), (b1, 1 - b0), (1 - b1, b0), (1 - b1, 1 - b0)]
    z_to = [device(x, y, zh, b2 * 4 + two * 2 + one, c) for two, one in quad]
    far = device(x, y, zh, (1 - b2) * 4 + b1 * 2 + b0, c)

    swap = device(y, x, zh, zl, c)
    t_to = [device(x, y, b2, zh * 4 + c * 2 + q, b1) for q in range(2)]
    stays = x == y
    same = jnp.logical_and(b2 == zh, b1 == c)

    barrier = pltpu.get_barrier_semaphore()

    def greet(target):
        pl.semaphore_signal(barrier, inc=1, device_id=target, device_id_type=MESH)

    for target in (sibling, anti, far, *a_to, *y_to[1:], *z_to[1:]):
        greet(target)

    @pl.when(jnp.logical_not(stays))
    def _():
        greet(swap)

    for q in range(2):

        @pl.when(jnp.logical_not(jnp.logical_and(same, b0 == q)))
        def _():
            greet(t_to[q])

    pl.semaphore_wait(barrier, 15 - jnp.where(stays, 1, 0) - jnp.where(same, 1, 0))

    live = {}

    def copy(name, src, dst, target):
        n = INDEX[name]
        return pltpu.make_async_remote_copy(
            src_ref=src, dst_ref=dst, send_sem=ss.at[n], recv_sem=rs.at[n], device_id=target, device_id_type=MESH
        )

    def begin(name, *rest):
        live[name] = copy(name, *rest)
        live[name].start()

    def chunk(p):
        return pl.ds(p * ROWS, ROWS)

    def start_cross(p):
        begin(f"cross{p}", w_ref.at[:, :, chunk(p)], wbuf.at[1, c, :, :, chunk(p)], anti)

    for p in range(min(AHEAD, PARTS)):
        start_cross(p)
    for n in range(3):
        begin(f"a{n + 1}", a_ref, abuf.at[x], a_to[n])
    begin("w", w_ref, wbuf.at[0, c], sibling)
    own_a = pltpu.make_async_copy(a_ref, abuf.at[x], ls.at[0])
    own_w = pltpu.make_async_copy(w_ref, wbuf.at[0, c], ls.at[1])
    own_a.start()
    own_w.start()
    own_a.wait()
    own_w.wait()
    for name in ("w", "a1", "a2", "a3"):
        live[name].wait_recv()

    def arrive(p):
        live[f"cross{p}"].wait_recv()
        if p + AHEAD < PARTS:
            start_cross(p + AHEAD)
        part = wbuf.at[1, c, :, :, chunk(p)]
        begin(f"cf{p}", part, part, sibling)

    low, high = pl.ds(0, 4 * ROWS), pl.ds(4 * ROWS, 4 * ROWS)

    def product(s):
        sel, p = s // PARTS, s % PARTS
        if sel:
            live[f"cf{p}"].wait_recv()

        def one(n, _):
            total = None
            for k in range(2):
                left = wbuf[sel, :, k, :, chunk(p)].reshape(8 * ROWS, 384)
                right = abuf[n, :, k].reshape(256, 384)
                part = lax.dot_general(left, right, (((1,), (1,)), ((), ())), preferred_element_type=F32)
                total = part if total is None else total + part
            t[s, n] = total
            return 0

        lax.fori_loop(0, 4, one, 0)
        direct = s in DIRECT
        y_send(s, 0, t[s, (y + 2) % 4, low], y_to[2 if direct else 1])
        y_send(s, 1, t[s, (y + 2) % 4, high], y_to[2 if direct else 3])
        y_send(s, 2, t[s, (y + 1) % 4, high], y_to[1])
        y_send(s, 3, t[s, (y + 3) % 4, low], y_to[3])
        if direct:
            y_send(s, 4, t[s, (y + 1) % 4, low], y_to[1])
            y_send(s, 5, t[s, (y + 3) % 4, high], y_to[3])

    def y_send(s, n, value, target):
        encode(y_out.at[s, n], value[: 2 * ROWS], value[2 * ROWS :])
        begin(f"y{n}{s}", y_out.at[s, n], y_in.at[s, n], target)

    def y_got(s, n):
        live[f"y{n}{s}"].wait_recv()
        return jnp.concatenate(decode(y_in.at[s, n]), axis=0)

    def y_pass(s):
        if s not in DIRECT:
            y_send(s, 4, y_got(s, 0) + t[s, (y + 1) % 4, low], y_to[1])
            y_send(s, 5, y_got(s, 1) + t[s, (y + 3) % 4, high], y_to[3])

    def y_end(s):
        first = t[s, y, low] + y_got(s, 3)
        second = t[s, y, high] + y_got(s, 2)
        if s in DIRECT:
            first += y_got(s, 0)
            second += y_got(s, 1)
        first += y_got(s, 4)
        second += y_got(s, 5)
        e[s, 0] = first.reshape(2, 2, ROWS, 256)
        e[s, 1] = second.reshape(2, 2, ROWS, 256)
        for n in (3, 2, 1):
            two, one = quad[n]
            encode(z_out.at[s, n - 1], e[s, two, one, 0], e[s, two, one, 1])
            begin(f"z{n}{s}", z_out.at[s, n - 1], z_in.at[s, n - 1], z_to[n])

    def z_end(s):
        sel, p = s // PARTS, s % PARTS
        first, second = e[s, b1, b0, 0], e[s, b1, b0, 1]
        for n in (1, 2, 3):
            live[f"z{n}{s}"].wait_recv()
            got = decode(z_in.at[s, n - 1])
            first, second = first + got[0], second + got[1]
        g[p, sel, 0] = first
        g[p, sel, 1] = second

        @pl.when(keep != sel)
        def _():
            encode(z4_out.at[p], g[p, sel, 0], g[p, sel, 1])
            copy(f"z4{p}", z4_out.at[p], z4.at[p], far).start()

    def swapped(p):
        return copy(f"sw{p}", gsum.at[p], drecv.at[:, chunk(p)], swap)

    def last(p):
        copy(f"z4{p}", z4_out.at[p], z4.at[p], far).wait_recv()
        got = decode(z4.at[p])
        gsum[p, 0] = g[p, keep, 0] + got[0]
        gsum[p, 1] = g[p, keep, 1] + got[1]

        @pl.when(stays)
        def _():
            drecv[:, chunk(p)] = gsum[p]

        @pl.when(jnp.logical_not(stays))
        def _():
            swapped(p).start()

        for q in range(2):
            itself = jnp.logical_and(same, b0 == q)

            @pl.when(itself)
            def _():
                rt[b0, :, chunk(p)] = gsum[p, :, :, q * 128 : (q + 1) * 128]

            @pl.when(jnp.logical_not(itself))
            def _():
                pltpu.make_async_remote_copy(
                    src_ref=gsum.at[p, :, :, pl.ds(q * 128, 128)],
                    dst_ref=rt.at[b0, :, chunk(p)],
                    send_sem=ss.at[INDEX[f"t{q}{p}"]],
                    recv_sem=rs.at[INDEX[f"t0{p}"] + b0],
                    device_id=t_to[q],
                    device_id_type=MESH,
                ).start()

    def finish(p):
        @pl.when(jnp.logical_not(stays))
        def _():
            swapped(p).wait()

        for q in range(2):

            @pl.when(jnp.logical_not(jnp.logical_and(same, b0 == q)))
            def _():
                copy(f"t{q}{p}", gsum.at[p, :, :, pl.ds(q * 128, 128)], rt.at[q, :, chunk(p)], t_to[q]).wait()

    what = dict(arrive=arrive, product=product, y_pass=y_pass, y_end=y_end, z_end=z_end, last=last, finish=finish)
    for name, n in plan():
        what[name](n)
    for one in live.values():
        one.wait_send()
    for p in range(PARTS):
        copy(f"z4{p}", z4_out.at[p], z4.at[p], far).wait_send()
    d = jnp.transpose(drecv[...].reshape(128, 256))
    o_ref[...] = (d + rt[...].reshape(256, 128)).astype(jnp.bfloat16)


def local(amplitudes, integrals):
    out = pl.pallas_call(
        kernel,
        out_shape=jax.ShapeDtypeStruct((256, 128), jnp.bfloat16),
        in_specs=[pl.BlockSpec(memory_space=pltpu.HBM)] * 2,
        out_specs=pl.BlockSpec(memory_space=pltpu.VMEM),
        scratch_shapes=[
            pltpu.VMEM((4, 4, 2, 64, 384), jnp.bfloat16),
            pltpu.VMEM((2, 2, 2, 4, 64, 384), jnp.bfloat16),
            pltpu.VMEM((STAGES, 4, 8 * ROWS, 256), F32),
            pltpu.VMEM((STAGES, 6, WORDS, 2 * ROWS, 256), WORD),
            pltpu.VMEM((STAGES, 6, WORDS, 2 * ROWS, 256), WORD),
            pltpu.VMEM((STAGES, 2, 2, 2, ROWS, 256), F32),
            pltpu.VMEM((STAGES, 3, WORDS, ROWS, 256), WORD),
            pltpu.VMEM((STAGES, 3, WORDS, ROWS, 256), WORD),
            pltpu.VMEM((PARTS, 2, 2, ROWS, 256), F32),
            pltpu.VMEM((PARTS, WORDS, ROWS, 256), WORD),
            pltpu.VMEM((PARTS, WORDS, ROWS, 256), WORD),
            pltpu.VMEM((PARTS, 2, ROWS, 256), F32),
            pltpu.VMEM((2, 64, 256), F32),
            pltpu.VMEM((2, 2, 64, 128), F32),
            pltpu.SemaphoreType.DMA((len(NAMES),)),
            pltpu.SemaphoreType.DMA((len(NAMES),)),
            pltpu.SemaphoreType.DMA((2,)),
        ],
        compiler_params=pltpu.CompilerParams(
            collective_id=0, has_side_effects=True, vmem_limit_bytes=48 * 1024 * 1024
        ),
    )(amplitudes, integrals)
    out = jnp.transpose(out.reshape(4, 64, 2, 64), (0, 2, 1, 3))
    return out.reshape(4, 2, 4096)


def solution(mesh):
    in_specs = (P("ia", "ja", None, None), P("ja", "ia", None, None))
    out_specs = P("ia", "ja", None)
    return jax.shard_map(local, mesh=mesh, in_specs=in_specs, out_specs=out_specs, check_vma=False)
```
